32 devices in a mesh: sec: 2 (over core), gx: 4 (over z), gy: 4 (over y, x).
Axes of the slice: x: 2, y: 2, z: 4, core: 2. Of those that a mesh axis runs over, the one named last changes fastest.
Arguments:
- air_sea_state: float32 [2, 16, 192, 1024], P('sec', None, 'gx', 'gy'), may hold values from -6 to 6
- diffusion: float32 [2, 16], P('sec'), may hold values from 0.04 to 0.15
- courant: float32 [2, 16], P('sec'), may hold values from 0.1 to 0.35
- exchange_coef: float32 [2, 192, 1024], P('sec', 'gx', 'gy'), may hold values from 0.2 to 1
- src_block: int32 [2, 3072], P('sec', ('gx', 'gy')), may hold values from 0 to 95
- dest_peer: int32 [2, 3072, 1], P('sec', ('gx', 'gy')), may hold values from 0 to 15; in each aligned block of 192 rows (0 to 191, 192 to 383, ..., all dimensions but the last counted through in order) at most 24 rows name the same one
- dest_block: int32 [2, 3072], P('sec', ('gx', 'gy')), may hold values from 0 to 95
- remap_weight: float32 [2, 3072, 128, 128], P('sec', ('gx', 'gy')), may hold values from -0.375 to 0.375
Outputs:
- new_state: float32 [2, 16, 192, 1024], P('sec', None, 'gx', 'gy')
- remapped: float32 [2, 4, 192, 1024], P('sec', None, 'gx', 'gy')
The draws below stay inside these ranges and needn't reach their ends.
Inputs may be any that keep to these rules, and one draw needn't show every extreme that they name: `dest_peer`: among the 192 entries owned by one device (aligned blocks of 192 entries of one component), no destination device is named more than 24 times, and in every draw some device is named exactly 24 times by some owner.
All inputs are finite; a program needn't handle non-finite values.
Results may differ from the reference program's by a relative error of at most 0.0001.
Values sent between devices are 32-bit elements; how exact they have to be, the bound alone decides.
A program may use at most 64 MiB of HBM per device.

```python
import math
import jax
import jax.numpy as jnp
import numpy as np
from jax import lax

COMPS = 2
LEV = 16
NF = 4
BLK = 128
CX = 48
CY = 256
STEPS_A = 6
STEPS_O = 3
OVL = 2
BPD = 96
EPD = 192
PEERS = 16
CAP = 24
ENTRIES = 3072
NX = 192
NY = 1024
N_GX = 4
N_GY = 4


def set_ends(drawn, stream_key, low, largest):
    extent = drawn.shape
    spot = [jax.random.randint(jax.random.fold_in(stream_key, axis), (), 0, extent[axis]) for axis in range(len(extent))]
    drawn = drawn.at[tuple(spot)].set(low)
    longest = extent.index(max(extent))
    spot[longest] = (spot[longest] + 1) % extent[longest]
    return drawn.at[tuple(spot)].set(largest)


def steps_of(own_key, dims, shards, least, largest):
    factor_of, own = 1.0, jax.random.fold_in(own_key, 6)
    for axis_at, shards_of in shards:
        heights = jnp.exp(jax.random.uniform(jax.random.fold_in(own, axis_at), (shards_of,), jnp.float32, least / len(shards), largest / len(shards)))
        factor_of = factor_of * jnp.repeat(heights, dims[axis_at] // shards_of).reshape([-1 if axis == axis_at else 1 for axis in range(len(dims))])
    return factor_of


def routed_block(rng, own, number, rows, number_of, top, bound, skew):
    sequence = jax.random.permutation(rng, number_of)
    packed, ordinary = shares(number_of, rows * top, bound, skew, True), shares(number_of, rows * top, bound, skew, False)
    places = jnp.arange(number_of)

    def named(sizes, rotation):
        used = int((sizes > 0).sum())
        fixed = max(1, used // 4)
        moved = fixed + (places - fixed + rotation * (used - fixed)) % max(1, number_of - fixed)
        return jnp.zeros((number_of,), jnp.int32).at[sequence[jnp.where(places < fixed, places, moved)]].set(jnp.asarray(sizes, jnp.int32))

    sizes = jnp.where(number % 4 == 0, named(packed, number // 4), named(ordinary, number - number // 4 - 1))
    mixed = jax.random.permutation(jax.random.fold_in(own, 3), number_of)
    source_of, sink = mixed[0:number_of // 2 * 2:2], mixed[1:number_of // 2 * 2:2]
    margin = jnp.minimum(sizes[source_of] - 1, bound - sizes[sink]) // 2
    margin = jnp.where((source_of == sequence[0]) | (sink == sequence[0]) | (sizes[sink] == 0), 0, jnp.maximum(margin, 0))
    moved = jax.random.randint(jax.random.fold_in(own, 4), (number_of // 2,), 0, 1 << 20) % (margin + 1)
    sizes = sizes.at[source_of].add(-moved).at[sink].add(moved)
    labels = jnp.searchsorted(jnp.cumsum(sizes), jnp.arange(rows * top), side="right").astype(jnp.int32)
    grid = labels.reshape(top, rows).T
    grid = grid[jax.random.permutation(jax.random.fold_in(own, 1), rows)]
    rotation = jax.random.randint(jax.random.fold_in(own, 2), (rows, 1), 0, top)
    return jnp.take_along_axis(grid, (jnp.arange(top)[None, :] + rotation) % top, axis=1)


def shares(count, total, most, skew, full):
    loads = [(1 << 20) // math.isqrt(standing ** skew) + 1 for standing in range(1, count + 1)]
    largest = most if full else min(most, max(-(-total // count), total * loads[0] // sum(loads)))
    least = 1 if total - largest >= count - 1 else 0
    counts, surplus = [largest] + [least] * (count - 1), total - largest - least * (count - 1)
    while surplus > 0:
        free = [i for i in range(1, count) if counts[i] < largest] or [i for i in range(1, count) if counts[i] < most]
        whole, left = sum([loads[i] for i in free]), surplus
        for i in free:
            extra = min(most - counts[i], max(1, left * loads[i] // whole), surplus)
            counts[i] = counts[i] + extra
            surplus = surplus - extra
    return np.array(counts)


def scatter_about(key, extent, deviation, most, pieces=(), kind=jnp.bfloat16):
    drawn = deviation * jax.random.normal(key, extent, jnp.float32)
    if pieces:
        drawn = drawn * steps_of(key, extent, pieces, -0.22, 0.18)
    return jnp.clip(drawn, -most, most).astype(kind)


def setup_inputs(seed: int = 0) -> dict:
    arg_keys = jax.random.split(jax.random.key(seed), 9)
    air_sea_state = scatter_about(arg_keys[0], (COMPS, LEV, NX, NY), 1.0, 6.0, ((0, 2), (2, 4), (3, 4)), jnp.float32)
    diffusion = jnp.clip(jnp.exp(math.log(0.15) - 1.3217559 * jax.random.uniform(arg_keys[1], (COMPS, LEV), jnp.float32) ** steps_of(arg_keys[1], (COMPS, LEV), ((0, 2),), -0.2, 0.2)), 0.04, 0.15)
    courant = jnp.clip(0.1 + 0.25 * jax.random.uniform(arg_keys[2], (COMPS, LEV), jnp.float32) ** steps_of(arg_keys[2], (COMPS, LEV), ((0, 2),), -0.2, 0.2), 0.1, 0.35)
    exchange_coef = jnp.clip(jnp.exp(math.log(1.0) - 1.609438 * jax.random.uniform(arg_keys[3], (COMPS, NX, NY), jnp.float32) ** steps_of(arg_keys[3], (COMPS, NX, NY), ((0, 2), (1, 4), (2, 4)), -0.2, 0.2)), 0.2, 1.0)
    src_block = set_ends(jax.random.randint(arg_keys[4], (COMPS, ENTRIES), 0, BPD), jax.random.fold_in(arg_keys[4], 1), 0, BPD - 1).astype(jnp.int32)
    dest_peer_keys = jax.random.split(jax.random.fold_in(arg_keys[5], 1), COMPS * ENTRIES // EPD)
    dest_peer_turns = jax.random.permutation(jax.random.fold_in(arg_keys[5], 3), COMPS * ENTRIES // EPD)
    dest_peer = jax.vmap(lambda own, number: routed_block(jax.random.fold_in(arg_keys[5], 2), own, number, EPD, PEERS, 1, CAP, 2))(dest_peer_keys, dest_peer_turns).reshape((COMPS, ENTRIES, 1))
    dest_block = set_ends(jax.random.randint(arg_keys[6], (COMPS, ENTRIES), 0, BPD), jax.random.fold_in(arg_keys[6], 1), 0, BPD - 1).astype(jnp.int32)
    remap_weight = scatter_about(arg_keys[7], (COMPS, ENTRIES, BLK, BLK), (BLK * OVL) ** -0.5, 0.375, ((0, 2), (1, 16)), jnp.float32)
    return dict(air_sea_state=air_sea_state, diffusion=diffusion, courant=courant, exchange_coef=exchange_coef, src_block=src_block, dest_peer=dest_peer, dest_block=dest_block, remap_weight=remap_weight)


def advance(levels, diffusion, courant):
    padded = jnp.pad(levels, ((0, 0), (0, 0), (1, 1), (1, 1)))
    prev_x = padded[:, :, :-2, 1:-1]
    beside_all = padded[:, :, 2:, 1:-1] + prev_x + padded[:, :, 1:-1, 2:] + padded[:, :, 1:-1, :-2]
    diffuse = diffusion[:, :, None, None]
    carry_rate = courant[:, :, None, None]
    return levels + diffuse * (beside_all - 4.0 * levels) - carry_rate * (levels - prev_x)


def to_blocks(surface):
    shaped = surface.reshape(NF, N_GX, CX, N_GY, CY // BLK, BLK)
    shaped = shaped.transpose(1, 3, 2, 4, 0, 5)
    return shaped.reshape(N_GX * N_GY * BPD, NF, BLK)


def from_blocks(totals):
    shaped = totals.reshape(N_GX, N_GY, CX, CY // BLK, NF, BLK)
    shaped = shaped.transpose(4, 0, 2, 1, 3, 5)
    return shaped.reshape(NF, CX * N_GX, CY * N_GY)


def reference(air_sea_state, diffusion, courant, exchange_coef, src_block, dest_peer, dest_block, remap_weight):
    stepped = air_sea_state
    for sweep_index in range(STEPS_A):
        candidate = advance(stepped, diffusion, courant)
        active = jnp.array([True, sweep_index < STEPS_O])[:, None, None, None]
        stepped = jnp.where(active, candidate, stepped)
    peer_count = N_GX * N_GY
    offsets = (jnp.arange(peer_count, dtype=jnp.int32) * BPD)[:, None]
    totals = [None, None]
    for comp in range(2):
        blocks = to_blocks(stepped[comp, :NF])
        tiles = remap_weight[comp].reshape(peer_count, EPD, BLK, BLK)
        source_rows = src_block[comp].reshape(peer_count, EPD).astype(jnp.int32) + offsets

        def owner_products(pair):
            tile_set, rows_now = pair
            picked = blocks[rows_now]
            return jnp.einsum("eij,efj->efi", tile_set, picked, precision=lax.Precision.HIGHEST)

        products = lax.map(owner_products, (tiles, source_rows)).reshape(peer_count * EPD, NF, BLK)
        target_rows = dest_peer[comp][:, 0].astype(jnp.int32) * BPD + dest_block[comp].astype(jnp.int32)
        totals[1 - comp] = jnp.zeros((peer_count * BPD, NF, BLK), jnp.float32).at[target_rows].add(products)
    remapped = jnp.stack([from_blocks(totals[0]), from_blocks(totals[1])])
    surface = stepped[:, :NF]
    coupling = exchange_coef[:, None]
    new_surface = surface + coupling * jnp.tanh(remapped - surface)
    new_state = jnp.concatenate([new_surface, stepped[:, NF:]], axis=1)
    return new_state, remapped
```

```python
import functools

import jax
import jax.numpy as jnp
from jax import lax
from jax.experimental import pallas as pl
from jax.experimental.pallas import tpu as pltpu
from jax.sharding import PartitionSpec as P

NF = 4
BLK = 128
STEPS_A = 6
STEPS_O = 3
HALO = 8
CHUNKS = 8
MESH = pl.DeviceIdType.MESH
F32 = jnp.float32
BF16 = jnp.bfloat16
SIDES = ((1, 0), (-1, 0), (0, 1), (0, -1), (1, 1), (1, -1), (-1, 1), (-1, -1))


def split_2(value):
    high = value.astype(BF16)
    return high, (value - high.astype(F32)).astype(BF16)


def dot_t(a, b):
    return lax.dot_general(a, b, (((1,), (1,)), ((), ())), preferred_element_type=F32)


def kernel(
    grid_x, grid_y, cap,
    state, diff, cour, coef, src_row, peer_row, block_row, w_hbm,
    new_state, remapped,
    w_f32, w_parts, rows_after, rows_before, edge_right, edge_left, cols_before, cols_after,
    inside, surf, table, take, picked, prods, pick, outgoing, incoming, lab_out, lab_in, spread,
    w_sem, halo_send, halo_recv, high_send, high_recv, lab_send, lab_recv, out_send, out_recv,
):
    sec, gx, gy = lax.axis_index("sec"), lax.axis_index("gx"), lax.axis_index("gy")
    peers = grid_x * grid_y
    me = gx * grid_y + gy
    levels, rows, cols = state.shape
    entries = peer_row.shape[1]
    blocks = rows * (cols // BLK)
    slots = peers * cap
    rows_ext, cols_ext = rows + 2 * HALO, cols + BLK
    per_chunk = entries * BLK // CHUNKS

    def w_copy(c):
        part = pl.ds(c * per_chunk, per_chunk)
        return pltpu.make_async_copy(w_hbm.at[part], w_f32.at[part], w_sem.at[c])

    for c in range(CHUNKS):
        w_copy(c).start()

    def there(side):
        dx, dy = side
        ok = jnp.bool_(True)
        if dx:
            ok = (gx < grid_x - 1) if dx > 0 else (gx > 0)
        if dy:
            ok_y = (gy < grid_y - 1) if dy > 0 else (gy > 0)
            ok = jnp.logical_and(ok, ok_y) if dx else ok_y
        return ok

    barrier = pltpu.get_barrier_semaphore()
    count = jnp.int32(peers)
    for dx, dy in SIDES:
        ok = there((dx, dy))
        count = count + jnp.where(ok, 1, 0)

        @pl.when(ok)
        def _(dx=dx, dy=dy):
            pl.semaphore_signal(
                barrier, inc=1, device_id=(sec, gx + dx, gy + dy), device_id_type=MESH
            )

    def other(k):
        p = lax.rem(me + k, peers)
        return p, (1 - sec, p // grid_y, lax.rem(p, grid_y))

    @pl.loop(0, peers)
    def _(k):
        pl.semaphore_signal(barrier, inc=1, device_id=other(k)[1], device_id_type=MESH)

    lane = lax.broadcasted_iota(jnp.int32, (rows, BLK), 1)

    def pack(l, carry):
        right, left = carry
        hit = (lane >= l * HALO) & (lane < l * HALO + HALO)
        last = state[l, :, cols - BLK :]
        first = state[l, :, :BLK]
        right = jnp.where(hit, pltpu.roll(last, l * HALO + HALO, 1), right)
        left = jnp.where(hit, pltpu.roll(first, l * HALO, 1), left)
        return right, left

    zero = jnp.zeros((rows, BLK), F32)
    right, left = (zero, zero)
    for l in range(levels):
        right, left = pack(l, (right, left))
    edge_right[...] = right
    edge_left[...] = left

    top, bottom = pl.ds(rows - HALO, HALO), pl.ds(0, HALO)
    below, above = pl.ds(rows, HALO), pl.ds(rows + HALO, HALO)
    low, high = pl.ds(0, NF), pl.ds(NF, levels - NF)
    everything = pl.ds(0, rows)
    ends = {
        (1, 0): (state.at[low, top], rows_before.at[low]),
        (-1, 0): (state.at[low, bottom], rows_after.at[low]),
        (0, 1): (edge_right.at[everything], cols_before.at[everything]),
        (0, -1): (edge_left.at[everything], cols_after.at[everything]),
        (1, 1): (edge_right.at[top], cols_before.at[above]),
        (1, -1): (edge_left.at[top], cols_after.at[above]),
        (-1, 1): (edge_right.at[bottom], cols_before.at[below]),
        (-1, -1): (edge_left.at[bottom], cols_after.at[below]),
    }
    for dx, dy in SIDES:
        dest = ends[dx, dy][1]

        @pl.when(jnp.logical_not(there((-dx, -dy))))
        def _(dx=dx, dy=dy, dest=dest):
            dest[...] = jnp.zeros(dest.shape, F32)
            if (dx, dy) == (1, 0):
                rows_before[NF:] = jnp.zeros((levels - NF, HALO, cols), F32)
            if (dx, dy) == (-1, 0):
                rows_after[NF:] = jnp.zeros((levels - NF, HALO, cols), F32)

    pl.semaphore_wait(barrier, count)

    def halo_copy(i):
        dx, dy = SIDES[i]
        source, dest = ends[dx, dy]
        return pltpu.make_async_remote_copy(
            src_ref=source, dst_ref=dest, send_sem=halo_send.at[i], recv_sem=halo_recv.at[i],
            device_id=(sec, gx + dx, gy + dy), device_id_type=MESH,
        )

    def high_copy(i):
        dx, dy = SIDES[i]
        source, dest = ((state.at[high, top], rows_before.at[high]),
                        (state.at[high, bottom], rows_after.at[high]))[i]
        return pltpu.make_async_remote_copy(
            src_ref=source, dst_ref=dest, send_sem=high_send.at[i], recv_sem=high_recv.at[i],
            device_id=(sec, gx + dx, gy + dy), device_id_type=MESH,
        )

    for i, side in enumerate(SIDES):
        pl.when(there(side))(lambda i=i: halo_copy(i).start())

    dest_row = peer_row[...].astype(F32)
    square = (entries, entries)
    e_row = lax.broadcasted_iota(jnp.int32, square, 1)
    e_col = lax.broadcasted_iota(jnp.int32, square, 0)
    wide = jnp.broadcast_to(dest_row, square)
    dest_col = jnp.sum(jnp.where(e_row == e_col, wide, 0.0), axis=1, keepdims=True)
    earlier = jnp.where((dest_col == wide) & (e_col < e_row), 1.0, 0.0)
    rank_row = jnp.sum(earlier, axis=0, keepdims=True)
    slot_row = (dest_row * cap + rank_row).astype(jnp.int32)
    pick[...] = jnp.where(
        lax.broadcasted_iota(jnp.int32, (slots, entries), 0) == slot_row, 1.0, 0.0
    ).astype(BF16)
    number = block_row[...]
    label = ((number % 2) * (blocks // 2) + number // 2 + 1).astype(F32)
    peer_at = lax.broadcasted_iota(jnp.int32, (peers, entries), 0)
    rank_at = lax.broadcasted_iota(jnp.int32, (BLK, entries), 0)
    source = src_row[...]
    source = ((source % 2) * (blocks // 2) + source // 2).astype(F32)
    source = jnp.sum(
        jnp.where(e_row == e_col, jnp.broadcast_to(source, square), 0.0), axis=1, keepdims=True
    )
    block_at = lax.broadcasted_iota(jnp.int32, (entries, blocks), 1)
    take[...] = jnp.where(block_at == source.astype(jnp.int32), 1.0, 0.0).astype(BF16)
    of_peer = jnp.where(peer_at == peer_row[...], label, 0.0).astype(BF16)
    of_rank = jnp.where(rank_at == rank_row.astype(jnp.int32), 1.0, 0.0).astype(BF16)
    labels = dot_t(of_peer, of_rank)
    lab_out[...] = jnp.broadcast_to(labels[:, None, :], lab_out.shape)

    def lab_copy(p, target, slot):
        return pltpu.make_async_remote_copy(
            src_ref=lab_out.at[p], dst_ref=lab_in.at[slot],
            send_sem=lab_send.at[p], recv_sem=lab_recv.at[slot],
            device_id=target, device_id_type=MESH,
        )

    def out_copy(p, target, slot):
        return pltpu.make_async_remote_copy(
            src_ref=outgoing.at[p], dst_ref=incoming.at[slot],
            send_sem=out_send.at[p], recv_sem=out_recv.at[slot],
            device_id=target, device_id_type=MESH,
        )

    @pl.loop(0, peers)
    def _(k):
        p, target = other(k)
        lab_copy(p, target, me).start()

    for i, side in enumerate(SIDES[:2]):
        pl.when(there(side))(lambda i=i: high_copy(i).start())

    shape_ext = (rows_ext, cols_ext)
    r = lax.broadcasted_iota(jnp.int32, shape_ext, 0)
    c = lax.broadcasted_iota(jnp.int32, shape_ext, 1)
    r = jnp.where(r < rows + HALO, r, r - rows_ext) + gx * rows
    near = (c < cols + HALO) | (c >= cols_ext - HALO)
    c = jnp.where(c < cols + HALO, c, c - cols_ext) + gy * cols
    ok = near & (r >= 0) & (r < grid_x * rows) & (c >= 0) & (c < grid_y * cols)
    inside[...] = jnp.where(ok, 1.0, 0.0)

    for chunk in range(CHUNKS):
        w_copy(chunk).wait()

        @pl.loop(0, per_chunk // BLK)
        def _(t, chunk=chunk):
            at = pl.ds(pl.multiple_of(chunk * per_chunk + t * BLK, BLK), BLK)
            part_high, part_low = split_2(w_f32[at, :])
            w_parts[at, :BLK] = part_high
            w_parts[at, BLK:] = part_low

    steps = jnp.where(sec == 0, STEPS_A, STEPS_O)
    side_lane = lax.broadcasted_iota(jnp.int32, (rows_ext, BLK), 1)

    def run(l):
        before = pltpu.roll(cols_before[...], BLK - HALO - l * HALO, 1)
        after = pltpu.roll(cols_after[...], lax.rem(BLK - l * HALO, BLK), 1)
        beside = jnp.where(
            side_lane < HALO, after, jnp.where(side_lane >= BLK - HALO, before, 0.0)
        )
        middle = jnp.concatenate([state[l], rows_after[l], rows_before[l]], axis=0)
        u = jnp.concatenate([middle, beside], axis=1)
        diffuse, carry_rate = diff[0, l], cour[0, l]

        def step(_, u):
            prev_x = pltpu.roll(u, 1, 0)
            around = (
                pltpu.roll(u, rows_ext - 1, 0) + prev_x
                + pltpu.roll(u, cols_ext - 1, 1) + pltpu.roll(u, 1, 1)
            )
            return u + inside[...] * (
                diffuse * (around - 4.0 * u) - carry_rate * (u - prev_x)
            )

        return lax.fori_loop(0, steps, step, u)[:rows, :cols]

    for i, (dx, dy) in enumerate(SIDES):
        pl.when(there((-dx, -dy)))(lambda i=i: halo_copy(i).wait_recv())

    for f in range(NF):
        u = run(jnp.int32(f))
        surf[f] = u
        part_high, part_low = split_2(u)
        for h in range(cols // BLK):
            at = slice(h * BLK, (h + 1) * BLK)
            of_block = slice(h * rows, (h + 1) * rows)
            table[of_block, f * BLK : (f + 1) * BLK] = part_high[:, at]
            table[of_block, (f + NF) * BLK : (f + NF + 1) * BLK] = part_low[:, at]

    gathered = jnp.dot(take[...], table[...], preferred_element_type=F32)
    for f in range(2 * NF):
        picked[pl.ds(f, entries, stride=2 * NF), :] = gathered[:, f * BLK : (f + 1) * BLK]

    @pl.loop(0, entries // 2, unroll=4)
    def _(g):
        left = picked[pl.ds(pl.multiple_of(g * 16, 16), 16), :].astype(BF16)
        left = jnp.concatenate([left, left], axis=1)
        out = dot_t(left, w_parts[pl.ds(pl.multiple_of(g * 2 * BLK, 2 * BLK), 2 * BLK), :])
        at = pl.multiple_of(g * 16, 16)
        prods[pl.ds(at, 8), :] = out[:8, :BLK]
        prods[pl.ds(at + 8, 8), :] = out[8:, BLK:]

    parts = []
    for f in range(NF):
        whole = prods[pl.ds(f, entries, stride=8), :] + prods[pl.ds(f + NF, entries, stride=8), :]
        parts.append(split_2(whole))
    both = jnp.concatenate([p for p, _ in parts] + [p for _, p in parts], axis=1)
    group = slots // grid_x

    @pl.loop(0, grid_x)
    def _(k):
        g = lax.rem(gx + 2 + k, grid_x)
        chosen = pick[pl.ds(pl.multiple_of(g * group, 16), group), :]
        found = jnp.dot(chosen, both, preferred_element_type=F32)
        for f in range(NF):
            value = found[:, f * BLK : (f + 1) * BLK] + found[:, (f + NF) * BLK : (f + NF + 1) * BLK]
            outgoing[pl.ds(g * grid_y, grid_y), f] = value.reshape(grid_y, cap, BLK)

        @pl.loop(0, grid_y)
        def _(j):
            to_y = lax.rem(gy + j, grid_y)
            out_copy(g * grid_y + to_y, (1 - sec, g, to_y), me).start()

    for i, (dx, dy) in enumerate(SIDES[:2]):
        pl.when(there((-dx, -dy)))(lambda i=i: high_copy(i).wait_recv())

    @pl.loop(NF, levels)
    def _(l):
        new_state[l] = run(l)

    @pl.loop(0, peers)
    def _(k):
        p, target = other(k)
        lab_copy(p, target, p).wait_recv()

    tall = jnp.concatenate([lab_in[...]] * (cap // 8), axis=1).reshape(slots, BLK)
    in_cap = lax.rem(lax.broadcasted_iota(jnp.int32, (slots, BLK), 0), cap)
    own = lax.broadcasted_iota(jnp.int32, (slots, BLK), 1) == in_cap
    tall = jnp.where(own, tall, 0.0).astype(BF16)
    label_at = dot_t(jnp.ones((blocks, BLK), BF16), tall)
    rows_at = lax.broadcasted_iota(jnp.int32, (blocks, slots), 0) + 1
    spread[...] = jnp.where(label_at.astype(jnp.int32) == rows_at, 1.0, 0.0).astype(BF16)

    @pl.loop(0, peers)
    def _(k):
        p, target = other(k)
        out_copy(p, target, p).wait_recv()

    for f in range(NF):
        came_high, came_low = split_2(incoming[:, f].reshape(slots, BLK))
        total = jnp.dot(spread[...], came_high, preferred_element_type=F32)
        total = total + jnp.dot(spread[...], came_low, preferred_element_type=F32)
        for h in range(cols // BLK):
            at = slice(h * BLK, (h + 1) * BLK)
            value = total[h * rows : (h + 1) * rows]
            remapped[f, :, at] = value
            now = surf[f, :, at]
            new_state[f, :, at] = now + coef[:, at] * jnp.tanh(value - now)

    for i, side in enumerate(SIDES):
        pl.when(there(side))(lambda i=i: halo_copy(i).wait_send())
    for i, side in enumerate(SIDES[:2]):
        pl.when(there(side))(lambda i=i: high_copy(i).wait_send())

    @pl.loop(0, peers)
    def _(k):
        p, target = other(k)
        lab_copy(p, target, me).wait_send()
        out_copy(p, target, me).wait_send()


def body(
    air_sea_state, diffusion, courant, exchange_coef, src_block, dest_peer, dest_block, remap_weight
):
    _, levels, rows, cols = air_sea_state.shape
    entries = remap_weight.shape[1]
    grid_x, grid_y = lax.axis_size("gx"), lax.axis_size("gy")
    peers = grid_x * grid_y
    cap = -(-max(2, 2 * entries // peers) // 8) * 8
    slots = peers * cap
    blocks = rows * (cols // BLK)
    vmem = pl.BlockSpec(memory_space=pltpu.VMEM)
    smem = pl.BlockSpec(memory_space=pltpu.SMEM)
    dma = pltpu.SemaphoreType.DMA
    new_state, remapped = pl.pallas_call(
        functools.partial(kernel, grid_x, grid_y, cap),
        name="coupled_interval",
        out_shape=(
            jax.ShapeDtypeStruct((levels, rows, cols), F32),
            jax.ShapeDtypeStruct((NF, rows, cols), F32),
        ),
        in_specs=[vmem, smem, smem, vmem, vmem, vmem, vmem, pl.BlockSpec(memory_space=pl.ANY)],
        out_specs=(vmem, vmem),
        scratch_shapes=[
            pltpu.VMEM((entries * BLK, BLK), F32),
            pltpu.VMEM((entries * BLK, 2 * BLK), BF16),
            pltpu.VMEM((levels, HALO, cols), F32),
            pltpu.VMEM((levels, HALO, cols), F32),
            pltpu.VMEM((rows, BLK), F32),
            pltpu.VMEM((rows, BLK), F32),
            pltpu.VMEM((rows + 2 * HALO, BLK), F32),
            pltpu.VMEM((rows + 2 * HALO, BLK), F32),
            pltpu.VMEM((rows + 2 * HALO, cols + BLK), F32),
            pltpu.VMEM((NF, rows, cols), F32),
            pltpu.VMEM((blocks, 2 * NF * BLK), BF16),
            pltpu.VMEM((entries, blocks), BF16),
            pltpu.VMEM((entries * 2 * NF, BLK), F32),
            pltpu.VMEM((entries * 2 * NF, BLK), F32),
            pltpu.VMEM((slots, entries), BF16),
            pltpu.VMEM((peers, NF, cap, BLK), F32),
            pltpu.VMEM((peers, NF, cap, BLK), F32),
            pltpu.VMEM((peers, 8, BLK), F32),
            pltpu.VMEM((peers, 8, BLK), F32),
            pltpu.VMEM((blocks, slots), BF16),
            dma((CHUNKS,)),
            dma((len(SIDES),)), dma((len(SIDES),)),
            dma((2,)), dma((2,)),
            dma((peers,)), dma((peers,)),
            dma((peers,)), dma((peers,)),
        ],
        compiler_params=pltpu.CompilerParams(
            collective_id=0, has_side_effects=True, vmem_limit_bytes=52 * 1024 * 1024
        ),
    )(
        air_sea_state[0],
        diffusion,
        courant,
        exchange_coef[0],
        src_block,
        dest_peer[:, :, 0],
        dest_block,
        remap_weight.reshape(entries * BLK, BLK),
    )
    return new_state[None], remapped[None]


def solution(mesh):
    in_specs = (
        P("sec", None, "gx", "gy"),
        P("sec", None),
        P("sec", None),
        P("sec", "gx", "gy"),
        P("sec", ("gx", "gy")),
        P("sec", ("gx", "gy"), None),
        P("sec", ("gx", "gy")),
        P("sec", ("gx", "gy"), None, None),
    )
    out_specs = (P("sec", None, "gx", "gy"), P("sec", None, "gx", "gy"))
    return jax.shard_map(body, mesh=mesh, in_specs=in_specs, out_specs=out_specs, check_vma=False)
```

```python
import functools

import jax
import jax.numpy as jnp
from jax import lax
from jax.experimental import pallas as pl
from jax.experimental.pallas import tpu as pltpu
from jax.sharding import PartitionSpec as P

NF = 4
BLK = 128
STEPS_A = 6
STEPS_O = 3
HALO = 8
CHUNKS = 8
MESH = pl.DeviceIdType.MESH
F32 = jnp.float32
BF16 = jnp.bfloat16
SIDES = ((1, 0), (-1, 0), (0, 1), (0, -1), (1, 1), (1, -1), (-1, 1), (-1, -1))


def split_2(value):
    high = value.astype(BF16)
    return high, (value - high.astype(F32)).astype(BF16)


def dot_t(a, b):
    return lax.dot_general(a, b, (((1,), (1,)), ((), ())), preferred_element_type=F32)


def kernel(
    grid_x, grid_y, cap,
    state_hbm, diff_hbm, cour_hbm, coef_hbm, src_hbm, peer_hbm, block_hbm, w_hbm,
    new_state, remapped,
    state, diff, cour, coef, src_row, peer_row, block_row,
    w_f32, w_parts, rows_after, rows_before, edge_right, edge_left, cols_before, cols_after,
    inside, surf, table, take, picked, prods, pick, outgoing, incoming, lab_out, lab_in, spread, total,
    in_sem, w_sem, halo_send, halo_recv, high_send, high_recv, lab_send, lab_recv, out_send, out_recv,
):
    sec, gx, gy = lax.axis_index("sec"), lax.axis_index("gx"), lax.axis_index("gy")
    peers = grid_x * grid_y
    me = gx * grid_y + gy
    levels, rows, cols = state.shape
    entries = peer_row.shape[1]
    blocks = rows * (cols // BLK)
    slots = peers * cap
    rows_ext, cols_ext = rows + 2 * HALO, cols + BLK
    per_chunk = entries * BLK // CHUNKS

    def w_copy(c):
        part = pl.ds(c * per_chunk, per_chunk)
        return pltpu.make_async_copy(w_hbm.at[part], w_f32.at[part], w_sem.at[c])

    small = [
        pltpu.make_async_copy(source, dest, in_sem.at[i])
        for i, (source, dest) in enumerate((
            (state_hbm, state), (peer_hbm, peer_row), (block_hbm, block_row), (src_hbm, src_row),
            (diff_hbm, diff), (cour_hbm, cour), (coef_hbm, coef),
        ))
    ]
    for copy in small:
        copy.start()
    for c in range(CHUNKS):
        w_copy(c).start()

    def there(side):
        dx, dy = side
        ok = jnp.bool_(True)
        if dx:
            ok = (gx < grid_x - 1) if dx > 0 else (gx > 0)
        if dy:
            ok_y = (gy < grid_y - 1) if dy > 0 else (gy > 0)
            ok = jnp.logical_and(ok, ok_y) if dx else ok_y
        return ok

    barrier = pltpu.get_barrier_semaphore()
    count = jnp.int32(peers)
    for dx, dy in SIDES:
        ok = there((dx, dy))
        count = count + jnp.where(ok, 1, 0)

        @pl.when(ok)
        def _(dx=dx, dy=dy):
            pl.semaphore_signal(
                barrier, inc=1, device_id=(sec, gx + dx, gy + dy), device_id_type=MESH
            )

    def other(k):
        p = lax.rem(me + k, peers)
        return p, (1 - sec, p // grid_y, lax.rem(p, grid_y))

    @pl.loop(0, peers)
    def _(k):
        pl.semaphore_signal(barrier, inc=1, device_id=other(k)[1], device_id_type=MESH)

    shape_ext = (rows_ext, cols_ext)
    r = lax.broadcasted_iota(jnp.int32, shape_ext, 0)
    c = lax.broadcasted_iota(jnp.int32, shape_ext, 1)
    r = jnp.where(r < rows + HALO, r, r - rows_ext) + gx * rows
    near = (c < cols + HALO) | (c >= cols_ext - HALO)
    c = jnp.where(c < cols + HALO, c, c - cols_ext) + gy * cols
    ok = near & (r >= 0) & (r < grid_x * rows) & (c >= 0) & (c < grid_y * cols)
    inside[...] = jnp.where(ok, 1.0, 0.0)

    for copy in small[1:]:
        copy.wait()

    dest_row = peer_row[...].astype(F32)
    square = (entries, entries)
    e_row = lax.broadcasted_iota(jnp.int32, square, 1)
    e_col = lax.broadcasted_iota(jnp.int32, square, 0)
    wide = jnp.broadcast_to(dest_row, square)
    dest_col = jnp.sum(jnp.where(e_row == e_col, wide, 0.0), axis=1, keepdims=True)
    earlier = jnp.where((dest_col == wide) & (e_col < e_row), 1.0, 0.0)
    rank_row = jnp.sum(earlier, axis=0, keepdims=True)
    slot_row = (dest_row * cap + rank_row).astype(jnp.int32)
    pick[...] = jnp.where(
        lax.broadcasted_iota(jnp.int32, (slots, entries), 0) == slot_row, 1.0, 0.0
    ).astype(BF16)
    number = block_row[...]
    label = ((number % 2) * (blocks // 2) + number // 2 + 1).astype(F32)
    peer_at = lax.broadcasted_iota(jnp.int32, (peers, entries), 0)
    rank_at = lax.broadcasted_iota(jnp.int32, (BLK, entries), 0)
    source = src_row[...]
    source = ((source % 2) * (blocks // 2) + source // 2).astype(F32)
    source = jnp.sum(
        jnp.where(e_row == e_col, jnp.broadcast_to(source, square), 0.0), axis=1, keepdims=True
    )
    block_at = lax.broadcasted_iota(jnp.int32, (entries, blocks), 1)
    take[...] = jnp.where(block_at == source.astype(jnp.int32), 1.0, 0.0).astype(BF16)
    of_peer = jnp.where(peer_at == peer_row[...], label, 0.0).astype(BF16)
    of_rank = jnp.where(rank_at == rank_row.astype(jnp.int32), 1.0, 0.0).astype(BF16)
    labels = dot_t(of_peer, of_rank)
    lab_out[...] = jnp.broadcast_to(labels[:, None, :], lab_out.shape)

    small[0].wait()

    lane = lax.broadcasted_iota(jnp.int32, (rows, BLK), 1)

    def pack(l, carry):
        right, left = carry
        hit = (lane >= l * HALO) & (lane < l * HALO + HALO)
        last = state[l, :, cols - BLK :]
        first = state[l, :, :BLK]
        right = jnp.where(hit, pltpu.roll(last, l * HALO + HALO, 1), right)
        left = jnp.where(hit, pltpu.roll(first, l * HALO, 1), left)
        return right, left

    zero = jnp.zeros((rows, BLK), F32)
    right, left = (zero, zero)
    for l in range(levels):
        right, left = pack(l, (right, left))
    edge_right[...] = right
    edge_left[...] = left

    top, bottom = pl.ds(rows - HALO, HALO), pl.ds(0, HALO)
    below, above = pl.ds(rows, HALO), pl.ds(rows + HALO, HALO)
    low, high = pl.ds(0, NF), pl.ds(NF, levels - NF)
    everything = pl.ds(0, rows)
    ends = {
        (1, 0): (state.at[low, top], rows_before.at[low]),
        (-1, 0): (state.at[low, bottom], rows_after.at[low]),
        (0, 1): (edge_right.at[everything], cols_before.at[everything]),
        (0, -1): (edge_left.at[everything], cols_after.at[everything]),
        (1, 1): (edge_right.at[top], cols_before.at[above]),
        (1, -1): (edge_left.at[top], cols_after.at[above]),
        (-1, 1): (edge_right.at[bottom], cols_before.at[below]),
        (-1, -1): (edge_left.at[bottom], cols_after.at[below]),
    }
    for dx, dy in SIDES:
        dest = ends[dx, dy][1]

        @pl.when(jnp.logical_not(there((-dx, -dy))))
        def _(dx=dx, dy=dy, dest=dest):
            dest[...] = jnp.zeros(dest.shape, F32)
            if (dx, dy) == (1, 0):
                rows_before[NF:] = jnp.zeros((levels - NF, HALO, cols), F32)
            if (dx, dy) == (-1, 0):
                rows_after[NF:] = jnp.zeros((levels - NF, HALO, cols), F32)

    pl.semaphore_wait(barrier, count)

    def halo_copy(i):
        dx, dy = SIDES[i]
        source, dest = ends[dx, dy]
        return pltpu.make_async_remote_copy(
            src_ref=source, dst_ref=dest, send_sem=halo_send.at[i], recv_sem=halo_recv.at[i],
            device_id=(sec, gx + dx, gy + dy), device_id_type=MESH,
        )

    def high_copy(i):
        dx, dy = SIDES[i]
        source, dest = ((state.at[high, top], rows_before.at[high]),
                        (state.at[high, bottom], rows_after.at[high]))[i]
        return pltpu.make_async_remote_copy(
            src_ref=source, dst_ref=dest, send_sem=high_send.at[i], recv_sem=high_recv.at[i],
            device_id=(sec, gx + dx, gy + dy), device_id_type=MESH,
        )

    for i, side in enumerate(SIDES):
        pl.when(there(side))(lambda i=i: halo_copy(i).start())

    def lab_copy(p, target, slot):
        return pltpu.make_async_remote_copy(
            src_ref=lab_out.at[p], dst_ref=lab_in.at[slot],
            send_sem=lab_send.at[p], recv_sem=lab_recv.at[slot],
            device_id=target, device_id_type=MESH,
        )

    def out_copy(p, target, slot):
        return pltpu.make_async_remote_copy(
            src_ref=outgoing.at[p], dst_ref=incoming.at[slot],
            send_sem=out_send.at[p], recv_sem=out_recv.at[slot],
            device_id=target, device_id_type=MESH,
        )

    @pl.loop(0, peers)
    def _(k):
        p, target = other(k)
        lab_copy(p, target, me).start()

    for i, side in enumerate(SIDES[:2]):
        pl.when(there(side))(lambda i=i: high_copy(i).start())

    for chunk in range(CHUNKS):
        w_copy(chunk).wait()

        @pl.loop(0, per_chunk // BLK)
        def _(t, chunk=chunk):
            at = pl.ds(pl.multiple_of(chunk * per_chunk + t * BLK, BLK), BLK)
            part_high, part_low = split_2(w_f32[at, :])
            w_parts[at, :BLK] = part_high
            w_parts[at, BLK:] = part_low

    steps = jnp.where(sec == 0, STEPS_A, STEPS_O)
    side_lane = lax.broadcasted_iota(jnp.int32, (rows_ext, BLK), 1)

    def run(l):
        before = pltpu.roll(cols_before[...], BLK - HALO - l * HALO, 1)
        after = pltpu.roll(cols_after[...], lax.rem(BLK - l * HALO, BLK), 1)
        beside = jnp.where(
            side_lane < HALO, after, jnp.where(side_lane >= BLK - HALO, before, 0.0)
        )
        middle = jnp.concatenate([state[l], rows_after[l], rows_before[l]], axis=0)
        u = jnp.concatenate([middle, beside], axis=1)
        diffuse, carry_rate = diff[0, l], cour[0, l]

        def step(_, u):
            prev_x = pltpu.roll(u, 1, 0)
            around = (
                pltpu.roll(u, rows_ext - 1, 0) + prev_x
                + pltpu.roll(u, cols_ext - 1, 1) + pltpu.roll(u, 1, 1)
            )
            return u + inside[...] * (
                diffuse * (around - 4.0 * u) - carry_rate * (u - prev_x)
            )

        return lax.fori_loop(0, steps, step, u)[:rows, :cols]

    for i, (dx, dy) in enumerate(SIDES):
        pl.when(there((-dx, -dy)))(lambda i=i: halo_copy(i).wait_recv())

    for f in range(NF):
        u = run(jnp.int32(f))
        surf[f] = u
        part_high, part_low = split_2(u)
        for h in range(cols // BLK):
            at = slice(h * BLK, (h + 1) * BLK)
            of_block = slice(h * rows, (h + 1) * rows)
            table[of_block, f * BLK : (f + 1) * BLK] = part_high[:, at]
            table[of_block, (f + NF) * BLK : (f + NF + 1) * BLK] = part_low[:, at]

    gathered = jnp.dot(take[...], table[...], preferred_element_type=F32)
    for f in range(2 * NF):
        picked[pl.ds(f, entries, stride=2 * NF), :] = gathered[:, f * BLK : (f + 1) * BLK]

    @pl.loop(0, entries // 2, unroll=16)
    def _(g):
        left = picked[pl.ds(pl.multiple_of(g * 16, 16), 16), :].astype(BF16)
        left = jnp.concatenate([left, left], axis=1)
        out = dot_t(left, w_parts[pl.ds(pl.multiple_of(g * 2 * BLK, 2 * BLK), 2 * BLK), :])
        at = pl.multiple_of(g * 16, 16)
        prods[pl.ds(at, 8), :] = out[:8, :BLK]
        prods[pl.ds(at + 8, 8), :] = out[8:, BLK:]

    parts = []
    for f in range(NF):
        whole = prods[pl.ds(f, entries, stride=8), :] + prods[pl.ds(f + NF, entries, stride=8), :]
        parts.append(split_2(whole))
    both = jnp.concatenate([p for p, _ in parts] + [p for _, p in parts], axis=1)
    group = slots // grid_x

    @pl.loop(0, grid_x)
    def _(k):
        g = lax.rem(gx // 2 + 1 + k // 2, grid_x // 2) * 2 + lax.rem(gx + k, 2)
        chosen = pick[pl.ds(pl.multiple_of(g * group, 16), group), :]
        found = jnp.dot(chosen, both, preferred_element_type=F32)
        for f in range(NF):
            value = found[:, f * BLK : (f + 1) * BLK] + found[:, (f + NF) * BLK : (f + NF + 1) * BLK]
            outgoing[pl.ds(g * grid_y, grid_y), f] = value.reshape(grid_y, cap, BLK)

        @pl.loop(0, grid_y)
        def _(j):
            to_y = lax.rem(gy + j, grid_y)
            out_copy(g * grid_y + to_y, (1 - sec, g, to_y), me).start()

    for i, (dx, dy) in enumerate(SIDES[:2]):
        pl.when(there((-dx, -dy)))(lambda i=i: high_copy(i).wait_recv())

    @pl.loop(NF, levels)
    def _(l):
        new_state[l] = run(l)

    @pl.loop(0, peers)
    def _(k):
        p, target = other(k)
        lab_copy(p, target, p).wait_recv()

    in_cap = lax.rem(lax.broadcasted_iota(jnp.int32, (group, BLK), 0), cap)
    own = lax.broadcasted_iota(jnp.int32, (group, BLK), 1) == in_cap
    rows_at = lax.broadcasted_iota(jnp.int32, (blocks, group), 0) + 1

    @pl.loop(0, grid_x)
    def _(g):
        tall = lab_in[pl.ds(g * grid_y, grid_y)]
        tall = jnp.concatenate([tall] * (cap // 8), axis=1).reshape(group, BLK)
        label_at = dot_t(jnp.ones((blocks, BLK), BF16), jnp.where(own, tall, 0.0).astype(BF16))
        spread[g] = jnp.where(label_at.astype(jnp.int32) == rows_at, 1.0, 0.0).astype(BF16)

    total[...] = jnp.zeros(total.shape, F32)

    @pl.loop(0, grid_x)
    def _(k):
        g = lax.rem(gx // 2 + k // 2, grid_x // 2) * 2 + lax.rem(gx + k, 2)

        @pl.loop(0, grid_y)
        def _(j):
            out_copy(g * grid_y + j, (1 - sec, g, j), g * grid_y + j).wait_recv()

        came = incoming[pl.ds(g * grid_y, grid_y)]
        parts = [split_2(came[:, f].reshape(group, BLK)) for f in range(NF)]
        both = jnp.concatenate([p for p, _ in parts] + [p for _, p in parts], axis=1)
        added = jnp.dot(spread[g], both, preferred_element_type=F32)
        total[...] += added[:, : NF * BLK] + added[:, NF * BLK :]

    for f in range(NF):
        for h in range(cols // BLK):
            at = slice(h * BLK, (h + 1) * BLK)
            value = total[h * rows : (h + 1) * rows, f * BLK : (f + 1) * BLK]
            remapped[f, :, at] = value
            now = surf[f, :, at]
            new_state[f, :, at] = now + coef[:, at] * jnp.tanh(value - now)

    for i, side in enumerate(SIDES):
        pl.when(there(side))(lambda i=i: halo_copy(i).wait_send())
    for i, side in enumerate(SIDES[:2]):
        pl.when(there(side))(lambda i=i: high_copy(i).wait_send())

    @pl.loop(0, peers)
    def _(k):
        p, target = other(k)
        lab_copy(p, target, me).wait_send()
        out_copy(p, target, me).wait_send()


def body(
    air_sea_state, diffusion, courant, exchange_coef, src_block, dest_peer, dest_block, remap_weight
):
    _, levels, rows, cols = air_sea_state.shape
    entries = remap_weight.shape[1]
    grid_x, grid_y = lax.axis_size("gx"), lax.axis_size("gy")
    peers = grid_x * grid_y
    cap = -(-max(2, 2 * entries // peers) // 8) * 8
    slots = peers * cap
    blocks = rows * (cols // BLK)
    vmem = pl.BlockSpec(memory_space=pltpu.VMEM)
    dma = pltpu.SemaphoreType.DMA
    new_state, remapped = pl.pallas_call(
        functools.partial(kernel, grid_x, grid_y, cap),
        name="coupled_interval",
        out_shape=(
            jax.ShapeDtypeStruct((levels, rows, cols), F32),
            jax.ShapeDtypeStruct((NF, rows, cols), F32),
        ),
        in_specs=[pl.BlockSpec(memory_space=pltpu.HBM)] * 8,
        out_specs=(vmem, vmem),
        scratch_shapes=[
            pltpu.VMEM((levels, rows, cols), F32),
            pltpu.SMEM((1, levels), F32),
            pltpu.SMEM((1, levels), F32),
            pltpu.VMEM((rows, cols), F32),
            pltpu.VMEM((1, entries), jnp.int32),
            pltpu.VMEM((1, entries), jnp.int32),
            pltpu.VMEM((1, entries), jnp.int32),
            pltpu.VMEM((entries * BLK, BLK), F32),
            pltpu.VMEM((entries * BLK, 2 * BLK), BF16),
            pltpu.VMEM((levels, HALO, cols), F32),
            pltpu.VMEM((levels, HALO, cols), F32),
            pltpu.VMEM((rows, BLK), F32),
            pltpu.VMEM((rows, BLK), F32),
            pltpu.VMEM((rows + 2 * HALO, BLK), F32),
            pltpu.VMEM((rows + 2 * HALO, BLK), F32),
            pltpu.VMEM((rows + 2 * HALO, cols + BLK), F32),
            pltpu.VMEM((NF, rows, cols), F32),
            pltpu.VMEM((blocks, 2 * NF * BLK), BF16),
            pltpu.VMEM((entries, blocks), BF16),
            pltpu.VMEM((entries * 2 * NF, BLK), F32),
            pltpu.VMEM((entries * 2 * NF, BLK), F32),
            pltpu.VMEM((slots, entries), BF16),
            pltpu.VMEM((peers, NF, cap, BLK), F32),
            pltpu.VMEM((peers, NF, cap, BLK), F32),
            pltpu.VMEM((peers, 8, BLK), F32),
            pltpu.VMEM((peers, 8, BLK), F32),
            pltpu.VMEM((grid_x, blocks, slots // grid_x), BF16),
            pltpu.VMEM((blocks, NF * BLK), F32),
            dma((7,)),
            dma((CHUNKS,)),
            dma((len(SIDES),)), dma((len(SIDES),)),
            dma((2,)), dma((2,)),
            dma((peers,)), dma((peers,)),
            dma((peers,)), dma((peers,)),
        ],
        compiler_params=pltpu.CompilerParams(
            collective_id=0, has_side_effects=True, vmem_limit_bytes=60 * 1024 * 1024
        ),
    )(
        air_sea_state[0],
        diffusion,
        courant,
        exchange_coef[0],
        src_block,
        dest_peer[:, :, 0],
        dest_block,
        remap_weight.reshape(entries * BLK, BLK),
    )
    return new_state[None], remapped[None]


def solution(mesh):
    in_specs = (
        P("sec", None, "gx", "gy"),
        P("sec", None),
        P("sec", None),
        P("sec", "gx", "gy"),
        P("sec", ("gx", "gy")),
        P("sec", ("gx", "gy"), None),
        P("sec", ("gx", "gy")),
        P("sec", ("gx", "gy"), None, None),
    )
    out_specs = (P("sec", None, "gx", "gy"), P("sec", None, "gx", "gy"))
    return jax.shard_map(body, mesh=mesh, in_specs=in_specs, out_specs=out_specs, check_vma=False)
```

```python
import functools

import jax
import jax.numpy as jnp
from jax import lax
from jax.experimental import pallas as pl
from jax.experimental.pallas import tpu as pltpu
from jax.sharding import PartitionSpec as P

NF = 4
BLK = 128
STEPS_A = 6
STEPS_O = 3
HALO = 8
CHUNKS = 8
MESH = pl.DeviceIdType.MESH
F32 = jnp.float32
BF16 = jnp.bfloat16
SIDES = ((1, 0), (-1, 0), (0, 1), (0, -1), (1, 1), (1, -1), (-1, 1), (-1, -1))


def split_2(value):
    high = value.astype(BF16)
    return high, (value - high.astype(F32)).astype(BF16)


def dot_t(a, b):
    return lax.dot_general(a, b, (((1,), (1,)), ((), ())), preferred_element_type=F32)


def kernel(
    grid_x, grid_y, cap,
    state_hbm, diff_hbm, cour_hbm, src_hbm, peer_hbm, block_hbm, w_hbm,
    surface_hbm, aloft_hbm, sum_high, sum_low,
    state, diff, cour, src_row, peer_row, block_row,
    w_f32, w_parts, rows_after, rows_before, edge_right, edge_left, cols_before, cols_after,
    inside, stepped, table, take, picked, prods, pick, outgoing, incoming, lab_out, lab_in, spread, total,
    in_sem, step_sem, w_sem, halo_send, halo_recv, high_send, high_recv, lab_send, lab_recv, out_send, out_recv,
):
    sec, gx, gy = lax.axis_index("sec"), lax.axis_index("gx"), lax.axis_index("gy")
    peers = grid_x * grid_y
    me = gx * grid_y + gy
    levels, rows, cols = state.shape
    entries = peer_row.shape[1]
    blocks = rows * (cols // BLK)
    slots = peers * cap
    rows_ext, cols_ext = rows + 2 * HALO, cols + BLK
    per_chunk = entries * BLK // CHUNKS

    def w_copy(c):
        part = pl.ds(c * per_chunk, per_chunk)
        return pltpu.make_async_copy(w_hbm.at[part], w_f32.at[part], w_sem.at[c])

    small = [
        pltpu.make_async_copy(source, dest, in_sem.at[i])
        for i, (source, dest) in enumerate((
            (state_hbm, state), (peer_hbm, peer_row), (block_hbm, block_row), (src_hbm, src_row),
            (diff_hbm, diff), (cour_hbm, cour),
        ))
    ]
    for copy in small:
        copy.start()
    for c in range(CHUNKS):
        w_copy(c).start()

    def there(side):
        dx, dy = side
        ok = jnp.bool_(True)
        if dx:
            ok = (gx < grid_x - 1) if dx > 0 else (gx > 0)
        if dy:
            ok_y = (gy < grid_y - 1) if dy > 0 else (gy > 0)
            ok = jnp.logical_and(ok, ok_y) if dx else ok_y
        return ok

    barrier = pltpu.get_barrier_semaphore()
    count = jnp.int32(peers)
    for dx, dy in SIDES:
        ok = there((dx, dy))
        count = count + jnp.where(ok, 1, 0)

        @pl.when(ok)
        def _(dx=dx, dy=dy):
            pl.semaphore_signal(
                barrier, inc=1, device_id=(sec, gx + dx, gy + dy), device_id_type=MESH
            )

    def other(k):
        p = lax.rem(me + k, peers)
        return p, (1 - sec, p // grid_y, lax.rem(p, grid_y))

    @pl.loop(0, peers)
    def _(k):
        pl.semaphore_signal(barrier, inc=1, device_id=other(k)[1], device_id_type=MESH)

    shape_ext = (rows_ext, cols_ext)
    r = lax.broadcasted_iota(jnp.int32, shape_ext, 0)
    c = lax.broadcasted_iota(jnp.int32, shape_ext, 1)
    r = jnp.where(r < rows + HALO, r, r - rows_ext) + gx * rows
    near = (c < cols + HALO) | (c >= cols_ext - HALO)
    c = jnp.where(c < cols + HALO, c, c - cols_ext) + gy * cols
    ok = near & (r >= 0) & (r < grid_x * rows) & (c >= 0) & (c < grid_y * cols)
    inside[...] = jnp.where(ok, 1.0, 0.0)

    for copy in small[1:]:
        copy.wait()

    dest_row = peer_row[...].astype(F32)
    square = (entries, entries)
    e_row = lax.broadcasted_iota(jnp.int32, square, 1)
    e_col = lax.broadcasted_iota(jnp.int32, square, 0)
    wide = jnp.broadcast_to(dest_row, square)
    dest_col = jnp.sum(jnp.where(e_row == e_col, wide, 0.0), axis=1, keepdims=True)
    earlier = jnp.where((dest_col == wide) & (e_col < e_row), 1.0, 0.0)
    rank_row = jnp.sum(earlier, axis=0, keepdims=True)
    slot_row = (dest_row * cap + rank_row).astype(jnp.int32)
    pick[...] = jnp.where(
        lax.broadcasted_iota(jnp.int32, (slots, entries), 0) == slot_row, 1.0, 0.0
    ).astype(BF16)
    number = block_row[...]
    label = ((number % 2) * (blocks // 2) + number // 2 + 1).astype(F32)
    peer_at = lax.broadcasted_iota(jnp.int32, (peers, entries), 0)
    rank_at = lax.broadcasted_iota(jnp.int32, (BLK, entries), 0)
    source = src_row[...]
    source = ((source % 2) * (blocks // 2) + source // 2).astype(F32)
    source = jnp.sum(
        jnp.where(e_row == e_col, jnp.broadcast_to(source, square), 0.0), axis=1, keepdims=True
    )
    block_at = lax.broadcasted_iota(jnp.int32, (entries, blocks), 1)
    take[...] = jnp.where(block_at == source.astype(jnp.int32), 1.0, 0.0).astype(BF16)
    of_peer = jnp.where(peer_at == peer_row[...], label, 0.0).astype(BF16)
    of_rank = jnp.where(rank_at == rank_row.astype(jnp.int32), 1.0, 0.0).astype(BF16)
    labels = dot_t(of_peer, of_rank)
    lab_out[...] = jnp.broadcast_to(labels[:, None, :], lab_out.shape)

    small[0].wait()

    lane = lax.broadcasted_iota(jnp.int32, (rows, BLK), 1)

    def pack(l, carry):
        right, left = carry
        hit = (lane >= l * HALO) & (lane < l * HALO + HALO)
        last = state[l, :, cols - BLK :]
        first = state[l, :, :BLK]
        right = jnp.where(hit, pltpu.roll(last, l * HALO + HALO, 1), right)
        left = jnp.where(hit, pltpu.roll(first, l * HALO, 1), left)
        return right, left

    zero = jnp.zeros((rows, BLK), F32)
    right, left = (zero, zero)
    for l in range(levels):
        right, left = pack(l, (right, left))
    edge_right[...] = right
    edge_left[...] = left

    top, bottom = pl.ds(rows - HALO, HALO), pl.ds(0, HALO)
    below, above = pl.ds(rows, HALO), pl.ds(rows + HALO, HALO)
    low, high = pl.ds(0, NF), pl.ds(NF, levels - NF)
    everything = pl.ds(0, rows)
    ends = {
        (1, 0): (state.at[low, top], rows_before.at[low]),
        (-1, 0): (state.at[low, bottom], rows_after.at[low]),
        (0, 1): (edge_right.at[everything], cols_before.at[everything]),
        (0, -1): (edge_left.at[everything], cols_after.at[everything]),
        (1, 1): (edge_right.at[top], cols_before.at[above]),
        (1, -1): (edge_left.at[top], cols_after.at[above]),
        (-1, 1): (edge_right.at[bottom], cols_before.at[below]),
        (-1, -1): (edge_left.at[bottom], cols_after.at[below]),
    }
    for dx, dy in SIDES:
        dest = ends[dx, dy][1]

        @pl.when(jnp.logical_not(there((-dx, -dy))))
        def _(dx=dx, dy=dy, dest=dest):
            dest[...] = jnp.zeros(dest.shape, F32)
            if (dx, dy) == (1, 0):
                rows_before[NF:] = jnp.zeros((levels - NF, HALO, cols), F32)
            if (dx, dy) == (-1, 0):
                rows_after[NF:] = jnp.zeros((levels - NF, HALO, cols), F32)

    pl.semaphore_wait(barrier, count)

    def halo_copy(i):
        dx, dy = SIDES[i]
        source, dest = ends[dx, dy]
        return pltpu.make_async_remote_copy(
            src_ref=source, dst_ref=dest, send_sem=halo_send.at[i], recv_sem=halo_recv.at[i],
            device_id=(sec, gx + dx, gy + dy), device_id_type=MESH,
        )

    def high_copy(i):
        dx, dy = SIDES[i]
        source, dest = ((state.at[high, top], rows_before.at[high]),
                        (state.at[high, bottom], rows_after.at[high]))[i]
        return pltpu.make_async_remote_copy(
            src_ref=source, dst_ref=dest, send_sem=high_send.at[i], recv_sem=high_recv.at[i],
            device_id=(sec, gx + dx, gy + dy), device_id_type=MESH,
        )

    for i, side in enumerate(SIDES):
        pl.when(there(side))(lambda i=i: halo_copy(i).start())

    def lab_copy(p, target, slot):
        return pltpu.make_async_remote_copy(
            src_ref=lab_out.at[p], dst_ref=lab_in.at[slot],
            send_sem=lab_send.at[p], recv_sem=lab_recv.at[slot],
            device_id=target, device_id_type=MESH,
        )

    def out_copy(p, target, slot):
        return pltpu.make_async_remote_copy(
            src_ref=outgoing.at[p], dst_ref=incoming.at[slot],
            send_sem=out_send.at[p], recv_sem=out_recv.at[slot],
            device_id=target, device_id_type=MESH,
        )

    @pl.loop(0, peers)
    def _(k):
        p, target = other(k)
        lab_copy(p, target, me).start()

    for i, side in enumerate(SIDES[:2]):
        pl.when(there(side))(lambda i=i: high_copy(i).start())

    for chunk in range(CHUNKS):
        w_copy(chunk).wait()

        @pl.loop(0, per_chunk // BLK, unroll=4)
        def _(t, chunk=chunk):
            at = pl.ds(pl.multiple_of(chunk * per_chunk + t * BLK, BLK), BLK)
            part_high, part_low = split_2(w_f32[at, :])
            w_parts[at, :BLK] = part_high
            w_parts[at, BLK:] = part_low

    steps = jnp.where(sec == 0, STEPS_A, STEPS_O)
    side_lane = lax.broadcasted_iota(jnp.int32, (rows_ext, BLK), 1)

    def run(l):
        before = pltpu.roll(cols_before[...], BLK - HALO - l * HALO, 1)
        after = pltpu.roll(cols_after[...], lax.rem(BLK - l * HALO, BLK), 1)
        beside = jnp.where(
            side_lane < HALO, after, jnp.where(side_lane >= BLK - HALO, before, 0.0)
        )
        middle = jnp.concatenate([state[l], rows_after[l], rows_before[l]], axis=0)
        u = jnp.concatenate([middle, beside], axis=1)
        diffuse, carry_rate = diff[0, l], cour[0, l]

        def step(_, u):
            prev_x = pltpu.roll(u, 1, 0)
            around = (
                pltpu.roll(u, rows_ext - 1, 0) + prev_x
                + pltpu.roll(u, cols_ext - 1, 1) + pltpu.roll(u, 1, 1)
            )
            return u + inside[...] * (
                diffuse * (around - 4.0 * u) - carry_rate * (u - prev_x)
            )

        return lax.fori_loop(0, steps, step, u)[:rows, :cols]

    for i, (dx, dy) in enumerate(SIDES):
        pl.when(there((-dx, -dy)))(lambda i=i: halo_copy(i).wait_recv())

    for f in range(NF):
        u = run(jnp.int32(f))
        stepped[f] = u
        part_high, part_low = split_2(u)
        for h in range(cols // BLK):
            at = slice(h * BLK, (h + 1) * BLK)
            of_block = slice(h * rows, (h + 1) * rows)
            table[of_block, f * BLK : (f + 1) * BLK] = part_high[:, at]
            table[of_block, (f + NF) * BLK : (f + NF + 1) * BLK] = part_low[:, at]

    gathered = jnp.dot(take[...], table[...], preferred_element_type=F32)
    for f in range(2 * NF):
        picked[pl.ds(f, entries, stride=2 * NF), :] = gathered[:, f * BLK : (f + 1) * BLK]

    @pl.loop(0, entries // 2, unroll=16)
    def _(g):
        left = picked[pl.ds(pl.multiple_of(g * 16, 16), 16), :].astype(BF16)
        left = jnp.concatenate([left, left], axis=1)
        out = dot_t(left, w_parts[pl.ds(pl.multiple_of(g * 2 * BLK, 2 * BLK), 2 * BLK), :])
        at = pl.multiple_of(g * 16, 16)
        prods[pl.ds(at, 8), :] = out[:8, :BLK]
        prods[pl.ds(at + 8, 8), :] = out[8:, BLK:]

    parts = []
    for f in range(NF):
        whole = prods[pl.ds(f, entries, stride=8), :] + prods[pl.ds(f + NF, entries, stride=8), :]
        parts.append(split_2(whole))
    both = jnp.concatenate([p for p, _ in parts] + [p for _, p in parts], axis=1)
    group = slots // grid_x

    @pl.loop(0, grid_x)
    def _(k):
        g = lax.rem(gx // 2 + 1 + k // 2, grid_x // 2) * 2 + lax.rem(gx + k, 2)
        chosen = pick[pl.ds(pl.multiple_of(g * group, 16), group), :]
        found = jnp.dot(chosen, both, preferred_element_type=F32)
        for f in range(NF):
            value = found[:, f * BLK : (f + 1) * BLK] + found[:, (f + NF) * BLK : (f + NF + 1) * BLK]
            outgoing[pl.ds(g * grid_y, grid_y), f] = value.reshape(grid_y, cap, BLK)

        @pl.loop(0, grid_y)
        def _(j):
            to_y = lax.rem(gy + j, grid_y)
            out_copy(g * grid_y + to_y, (1 - sec, g, to_y), me).start()

    for i, (dx, dy) in enumerate(SIDES[:2]):
        pl.when(there((-dx, -dy)))(lambda i=i: high_copy(i).wait_recv())

    @pl.loop(NF, levels)
    def _(l):
        stepped[l] = run(l)

    keep = (
        pltpu.make_async_copy(stepped.at[low], surface_hbm, step_sem.at[0]),
        pltpu.make_async_copy(stepped.at[high], aloft_hbm, step_sem.at[1]),
    )
    for copy in keep:
        copy.start()

    @pl.loop(0, peers)
    def _(k):
        p, target = other(k)
        lab_copy(p, target, p).wait_recv()

    in_cap = lax.rem(lax.broadcasted_iota(jnp.int32, (group, BLK), 0), cap)
    own = lax.broadcasted_iota(jnp.int32, (group, BLK), 1) == in_cap
    rows_at = lax.broadcasted_iota(jnp.int32, (blocks, group), 0) + 1

    @pl.loop(0, grid_x)
    def _(g):
        tall = lab_in[pl.ds(g * grid_y, grid_y)]
        tall = jnp.concatenate([tall] * (cap // 8), axis=1).reshape(group, BLK)
        label_at = dot_t(jnp.ones((blocks, BLK), BF16), jnp.where(own, tall, 0.0).astype(BF16))
        spread[g] = jnp.where(label_at.astype(jnp.int32) == rows_at, 1.0, 0.0).astype(BF16)

    total[...] = jnp.zeros(total.shape, F32)

    @pl.loop(0, grid_x)
    def _(k):
        g = lax.rem(gx // 2 + k // 2, grid_x // 2) * 2 + lax.rem(gx + k, 2)

        @pl.loop(0, grid_y)
        def _(j):
            out_copy(g * grid_y + j, (1 - sec, g, j), g * grid_y + j).wait_recv()

        came = incoming[pl.ds(g * grid_y, grid_y)]
        parts = [split_2(came[:, f].reshape(group, BLK)) for f in range(NF)]
        both = jnp.concatenate([p for p, _ in parts] + [p for _, p in parts], axis=1)
        added = jnp.dot(spread[g], both, preferred_element_type=F32)
        total[...] += added

    for f in range(NF):
        for h in range(cols // BLK):
            at = slice(h * BLK, (h + 1) * BLK)
            of_block = slice(h * rows, (h + 1) * rows)
            sum_high[f, :, at] = total[of_block, f * BLK : (f + 1) * BLK]
            sum_low[f, :, at] = total[of_block, (f + NF) * BLK : (f + NF + 1) * BLK]

    for copy in keep:
        copy.wait()
    for i, side in enumerate(SIDES):
        pl.when(there(side))(lambda i=i: halo_copy(i).wait_send())
    for i, side in enumerate(SIDES[:2]):
        pl.when(there(side))(lambda i=i: high_copy(i).wait_send())

    @pl.loop(0, peers)
    def _(k):
        p, target = other(k)
        lab_copy(p, target, me).wait_send()
        out_copy(p, target, me).wait_send()


def body(
    air_sea_state, diffusion, courant, exchange_coef, src_block, dest_peer, dest_block, remap_weight
):
    _, levels, rows, cols = air_sea_state.shape
    entries = remap_weight.shape[1]
    grid_x, grid_y = lax.axis_size("gx"), lax.axis_size("gy")
    peers = grid_x * grid_y
    cap = -(-max(2, 2 * entries // peers) // 8) * 8
    slots = peers * cap
    blocks = rows * (cols // BLK)
    vmem = pl.BlockSpec(memory_space=pltpu.VMEM)
    dma = pltpu.SemaphoreType.DMA
    surface, aloft, sum_high, sum_low = pl.pallas_call(
        functools.partial(kernel, grid_x, grid_y, cap),
        name="coupled_interval",
        out_shape=(
            jax.ShapeDtypeStruct((NF, rows, cols), F32),
            jax.ShapeDtypeStruct((levels - NF, rows, cols), F32),
            jax.ShapeDtypeStruct((NF, rows, cols), F32),
            jax.ShapeDtypeStruct((NF, rows, cols), F32),
        ),
        in_specs=[pl.BlockSpec(memory_space=pltpu.HBM)] * 7,
        out_specs=(pl.BlockSpec(memory_space=pltpu.HBM), pl.BlockSpec(memory_space=pltpu.HBM), vmem, vmem),
        scratch_shapes=[
            pltpu.VMEM((levels, rows, cols), F32),
            pltpu.SMEM((1, levels), F32),
            pltpu.SMEM((1, levels), F32),
            pltpu.VMEM((1, entries), jnp.int32),
            pltpu.VMEM((1, entries), jnp.int32),
            pltpu.VMEM((1, entries), jnp.int32),
            pltpu.VMEM((entries * BLK, BLK), F32),
            pltpu.VMEM((entries * BLK, 2 * BLK), BF16),
            pltpu.VMEM((levels, HALO, cols), F32),
            pltpu.VMEM((levels, HALO, cols), F32),
            pltpu.VMEM((rows, BLK), F32),
            pltpu.VMEM((rows, BLK), F32),
            pltpu.VMEM((rows + 2 * HALO, BLK), F32),
            pltpu.VMEM((rows + 2 * HALO, BLK), F32),
            pltpu.VMEM((rows + 2 * HALO, cols + BLK), F32),
            pltpu.VMEM((levels, rows, cols), F32),
            pltpu.VMEM((blocks, 2 * NF * BLK), BF16),
            pltpu.VMEM((entries, blocks), BF16),
            pltpu.VMEM((entries * 2 * NF, BLK), F32),
            pltpu.VMEM((entries * 2 * NF, BLK), F32),
            pltpu.VMEM((slots, entries), BF16),
            pltpu.VMEM((peers, NF, cap, BLK), F32),
            pltpu.VMEM((peers, NF, cap, BLK), F32),
            pltpu.VMEM((peers, 8, BLK), F32),
            pltpu.VMEM((peers, 8, BLK), F32),
            pltpu.VMEM((grid_x, blocks, slots // grid_x), BF16),
            pltpu.VMEM((blocks, 2 * NF * BLK), F32),
            dma((6,)),
            dma((2,)),
            dma((CHUNKS,)),
            dma((len(SIDES),)), dma((len(SIDES),)),
            dma((2,)), dma((2,)),
            dma((peers,)), dma((peers,)),
            dma((peers,)), dma((peers,)),
        ],
        compiler_params=pltpu.CompilerParams(
            collective_id=0, has_side_effects=True, vmem_limit_bytes=60 * 1024 * 1024
        ),
    )(
        air_sea_state[0],
        diffusion,
        courant,
        src_block,
        dest_peer[:, :, 0],
        dest_block,
        remap_weight.reshape(entries * BLK, BLK),
    )
    remapped = sum_high + sum_low
    surface = surface + exchange_coef * jnp.tanh(remapped - surface)
    new_state = jnp.concatenate([surface, aloft], axis=0)
    return new_state[None], remapped[None]


def solution(mesh):
    in_specs = (
        P("sec", None, "gx", "gy"),
        P("sec", None),
        P("sec", None),
        P("sec", "gx", "gy"),
        P("sec", ("gx", "gy")),
        P("sec", ("gx", "gy"), None),
        P("sec", ("gx", "gy")),
        P("sec", ("gx", "gy"), None, None),
    )
    out_specs = (P("sec", None, "gx", "gy"), P("sec", None, "gx", "gy"))
    return jax.shard_map(body, mesh=mesh, in_specs=in_specs, out_specs=out_specs, check_vma=False)
```
